512 devices in a mesh: va: 32 (over x, z_lo), vb: 16 (over y, z_hi, core).
Axes of the slice: x: 4, y: 4, z: 16 (z_hi: 2, z_lo: 8; z = z_hi * 8 + z_lo), core: 2. Of those that a mesh axis runs over, the one named last changes fastest.
Arguments:
- lam: bfloat16 [4, 6144, 6144], P(None, 'va', 'vb'), may hold values from -6 to 6
- fock_vv: bfloat16 [6144, 6144], P('va', 'vb'), may hold values from -0.078125 to 0.078125
- amp: bfloat16 [4, 6144, 6144], P(None, 'va', 'vb'), may hold values from -6 to 6
- tile_mask: int32 [4, 64, 64], P(None, 'va', 'vb'), may hold values 0 or 1
- integrals: bfloat16 [4, 6144, 6144], P(None, 'va', 'vb'), may hold values from -6 to 6
Outputs:
- residual: bfloat16 [4, 6144, 6144], P(None, 'va', 'vb')
The draws below stay inside these ranges and needn't reach their ends.
All inputs are finite; a program needn't handle non-finite values. No bound on the sum of `tile_mask` on one device may be relied on, other than what follows from the above.
Results may differ from the reference program's by a relative error of at most 0.001.
Values may be sent and summed in bfloat16 or wider, within the bound.
A program may use at most 64 MiB of HBM per device.

```python
import jax
import jax.numpy as jnp
from jax import lax

VIRT = 6144
TILE = 96
PAIRS = 4
NTILE = 64


def place_ends(drawn, own_key, least, high):
    longest = drawn.shape.index(max(drawn.shape))
    spots = []
    for shift in (0, 1):
        where = [jax.random.randint(jax.random.fold_in(own_key, axis), (), 0, length) for axis, length in enumerate(drawn.shape)]
        where[longest] = (where[longest] + shift) % drawn.shape[longest]
        spots.append(tuple(where))
    return drawn.at[spots[0]].set(least).at[spots[1]].set(high)


def block_scale(key, extent, cuts, least, top_value):
    factor_of = 1.0
    for dim, shards_of in cuts:
        steps = jax.random.uniform(jax.random.fold_in(jax.random.fold_in(key, 6), dim), (shards_of,), jnp.float32, least / len(cuts), top_value / len(cuts))
        factor_of = factor_of * jnp.repeat(jnp.exp(steps), extent[dim] // shards_of).reshape((-1,) + (1,) * (len(extent) - 1 - dim))
    return factor_of


def bell_draw(own_key, shape, deviation, reach, shards=(), held_as=jnp.bfloat16):
    entries = jax.random.normal(own_key, shape, jnp.float32) * deviation
    if len(shards) > 0:
        entries = block_scale(own_key, shape, shards, -0.22, 0.18) * entries
    return jnp.clip(entries, min=-reach, max=reach).astype(held_as)


def setup_inputs(seed: int = 0) -> dict:
    streams_of = jax.random.split(jax.random.key(seed), 6)
    return {
        "lam": bell_draw(streams_of[0], (PAIRS, VIRT, VIRT), 1.0, 6.0, ((1, 32), (2, 16))),
        "fock_vv": bell_draw(streams_of[1], (VIRT, VIRT), VIRT ** -0.5, 0.078125, ((0, 32), (1, 16))),
        "amp": bell_draw(streams_of[2], (PAIRS, VIRT, VIRT), 1.0, 6.0, ((1, 32), (2, 16))),
        "tile_mask": place_ends((jax.random.randint(streams_of[3], (PAIRS, NTILE, NTILE), 0, 2) < 1).astype(jnp.int32), jax.random.fold_in(streams_of[3], 1), 0, 1),
        "integrals": bell_draw(streams_of[4], (PAIRS, VIRT, VIRT), 1.0, 6.0, ((1, 32), (2, 16))),
    }


def expand_mask(tile_mask):
    widened = jnp.repeat(jnp.repeat(tile_mask, TILE, axis=1), TILE, axis=2)
    return widened.astype(jnp.bfloat16)


def reference(lam, fock_vv, amp, tile_mask, integrals):
    screened = amp * expand_mask(tile_mask)
    flat_lam = lam.reshape(PAIRS, -1)
    flat_amp = screened.reshape(PAIRS, -1)
    intersection = jnp.dot(flat_lam, flat_amp.T, preferred_element_type=jnp.float32) / VIRT
    ladder = jnp.dot(intersection, integrals.reshape(PAIRS, -1).astype(jnp.float32), precision=lax.Precision.HIGHEST)
    ladder = ladder.reshape(PAIRS, VIRT, VIRT)

    def one_pair(pair_block):
        return jnp.dot(pair_block, fock_vv, preferred_element_type=jnp.float32)

    one_body = lax.map(one_pair, lam)
    total_sum = integrals.astype(jnp.float32) + one_body + ladder
    return total_sum.astype(jnp.bfloat16)
```

```python
import functools

import jax
import jax.numpy as jnp
from jax import lax
from jax.experimental import pallas as pl
from jax.experimental.pallas import tpu as pltpu
from jax.sharding import PartitionSpec as P

VIRT = 6144
PAIRS = 4
RA = 192
CB = 384
ROWS = PAIRS * RA
HALF = RA // 2
MESH = pl.DeviceIdType.MESH

NU = 4
LAM_START = (0, 3, 6, 9)
FOCK_START = (0, 2)
STEPS = LAM_START[-1] + 8

SUM_STEPS = (
    (0, 0, 0, 1),
    (0, 1, 0, 0),
    (0, 2, 0, 0),
    (1, 0, 0, 0),
    (2, 0, 0, 0),
    (0, 0, 1, 0),
    (0, 0, 2, 0),
    (0, 0, 4, 0),
    (0, 0, 8, 0),
)


def kernel(
    lam_ref, fock_ref, amp_ref, mask_ref, int_ref, out_ref,
    L, F, T, A, I, acc, O, sbuf, rbuf,
    in_sem, lam_rs, fock_rs, fock_ss, x_rs, y0_rs, y1_rs, c0_rs, c1_rs, sum_rs, sum_ss,
    zs_sem, xs_sem, ys_sem, cs_sem, out_sem,
):
    va, vb = lax.axis_index("va"), lax.axis_index("vb")
    x, zl = va // 8, va % 8
    y, zh, c = vb // 4, (vb // 2) % 2, vb % 2
    z = zh * 8 + zl

    def dev(dx, dy, dz, dc):
        xx, yy, zz, cc = (x + dx) % 4, (y + dy) % 4, (z + dz) % 16, (c + dc) % 2
        return (xx * 8 + zz % 8, (yy * 2 + zz // 8) * 2 + cc)

    def remote(src, dst, ss, rs, to):
        pltpu.make_async_remote_copy(src, dst, ss, rs, device_id=dev(*to), device_id_type=MESH).start()

    def wait(ref, sem):
        pltpu.make_async_copy(ref, ref, sem).wait()

    own = vb
    far = (y * 2 + (1 - zh)) * 2 + c

    def frows(zsrc, f=None):
        base = (x * 8 + zsrc) * RA
        if f is None:
            return F.at[pl.ds(pl.multiple_of(base, RA), RA)]
        return F.at[pl.ds(pl.multiple_of(base + f * HALF, HALF), HALF)]

    def lrows(b, u, d):
        return L.at[b, pl.ds(u * RA + d * HALF, HALF)]

    cp_lam = pltpu.make_async_copy(lam_ref, L.at[own], in_sem.at[0])
    cp_fock = pltpu.make_async_copy(fock_ref, frows(zl), in_sem.at[1])
    cp_amp = pltpu.make_async_copy(amp_ref, A, in_sem.at[2])
    cp_int = pltpu.make_async_copy(int_ref, I, in_sem.at[3])
    cp_lam.start()
    cp_fock.start()
    cp_amp.start()
    cp_int.start()

    peers = set()
    for o in SUM_STEPS + ((0, 3, 0, 0), (3, 0, 0, 0), (0, 0, 15, 0)):
        peers.add(o)
        peers.add(((-o[0]) % 4, (-o[1]) % 4, (-o[2]) % 16, (-o[3]) % 2))
    peers = sorted(peers)
    bar = pltpu.get_barrier_semaphore()
    for o in peers:
        pl.semaphore_signal(bar, inc=1, device_id=dev(*o), device_id_type=MESH)
    pl.semaphore_wait(bar, len(peers))

    DZ = ((0, 0, 1, 0), (0, 0, -1, 0))
    SG = (1, -1)

    def lam_send(d, u, h):
        src = lrows(own, u, d) if h == 0 else T.at[d, u, h - 1]
        if h < 7:
            dst = T.at[d, u, h]
        else:
            zz = (z + SG[d]) % 16
            dst = lrows((y * 2 + (1 - zz // 8)) * 2 + c, u, d)
        remote(src, dst, zs_sem, lam_rs.at[d, u, h], DZ[d])

    def lam_wait(d, u, h):
        wait(T.at[d, u, h] if h < 7 else lrows(far, u, d), lam_rs.at[d, u, h])

    def fock_send(d, f, h):
        s = SG[d]
        zsrc = zl - s * h

        @pl.when((zsrc >= 0) & (zsrc < 8) & (zl + s >= 0) & (zl + s < 8))
        def _():
            blk = frows(zsrc, f)
            remote(blk, blk, fock_ss.at[d, f, h], fock_rs.at[d, f, h], DZ[d])

    def fock_arrive(d, f, h):
        s = SG[d]
        zsrc = zl - s * (h + 1)

        @pl.when((zsrc >= 0) & (zsrc < 8))
        def _():
            blk = frows(zsrc, f)
            wait(blk, fock_rs.at[d, f, h])

        if h < 6:
            fock_send(d, f, h + 1)

        @pl.when((zsrc >= 0) & (zsrc < 8))
        def _():
            blk = frows(zsrc, f)
            for dx in (1, 3, 2):
                remote(blk, blk, xs_sem, x_rs, (dx, 0, 0, 0))

    cp_lam.wait()
    cp_fock.wait()
    for u in range(NU):
        if LAM_START[u] == 0:
            for d in (0, 1):
                lam_send(d, u, 0)
    for f in (0, 1):
        if FOCK_START[f] == 0:
            for d in (0, 1):
                fock_send(d, f, 0)
    blk = frows(zl)
    for dx in (1, 3, 2):
        remote(blk, blk, xs_sem, x_rs, (dx, 0, 0, 0))
    for dy in (1, 3, 2):
        remote(L.at[own], L.at[own], ys_sem, y0_rs.at[dy - 1], (0, dy, 0, 0))
    remote(L.at[own], L.at[own], cs_sem, c0_rs, (0, 0, 0, 1))

    cp_amp.wait()
    col = lax.broadcasted_iota(jnp.int32, (1, CB), 1) // HALF
    row8 = lax.broadcasted_iota(jnp.int32, (8, 128), 0)
    col8 = lax.broadcasted_iota(jnp.int32, (8, 128), 1)
    part = jnp.zeros((8, 128), jnp.float32)
    for q in range(PAIRS):
        sums = tuple(jnp.zeros((16, CB), jnp.float32) for _ in range(PAIRS))
        for i in range(2):
            wide = jnp.zeros((1, CB), jnp.float32)
            for j in range(4):
                kept = mask_ref[q, i, j].astype(jnp.float32)
                wide = wide + kept * (col == j).astype(jnp.float32)

            def rows16(k, sums, i=i, q=q, wide=wide):
                r = pl.multiple_of(i * HALF + k * 16, 16)
                a = A[pl.ds(q * RA + r, 16), :].astype(jnp.float32) * wide
                return tuple(
                    s + L[own, pl.ds(p * RA + r, 16), :].astype(jnp.float32) * a for p, s in enumerate(sums)
                )

            sums = lax.fori_loop(0, HALF // 16, rows16, sums)
        for p in range(PAIRS):
            part = part + jnp.where((row8 == p) & (col8 == q), jnp.sum(sums[p]), 0.0)
    sbuf[0] = part
    remote(sbuf.at[0], rbuf.at[0], sum_ss.at[0], sum_rs.at[0], SUM_STEPS[0])

    def sum_step(k):
        wait(rbuf.at[k], sum_rs.at[k])
        sbuf[k + 1] = sbuf[k] + rbuf[k]
        if k + 1 < len(SUM_STEPS):
            remote(sbuf.at[k + 1], rbuf.at[k + 1], sum_ss.at[k + 1], sum_rs.at[k + 1], SUM_STEPS[k + 1])

    def base():
        cp_int.wait()
        inter = sbuf[len(SUM_STEPS)] / VIRT

        def rows16(k, carry):
            r = pl.multiple_of(k * 16, 16)
            g = [I[pl.ds(q * RA + r, 16), :].astype(jnp.float32) for q in range(PAIRS)]
            for p in range(PAIRS):
                t = g[p]
                for q in range(PAIRS):
                    t = t + inter[p : p + 1, q : q + 1] * g[q]
                acc[pl.ds(p * RA + r, 16), :] = t
            return carry

        lax.fori_loop(0, RA // 16, rows16, 0)

    def y0_arrive(dy):
        b = (((y - dy) % 4) * 2 + zh) * 2 + c
        wait(L.at[b], y0_rs.at[dy - 1])
        remote(L.at[b], L.at[b], cs_sem, c0_rs, (0, 0, 0, 1))

    def lam_final(d, u):
        blk = lrows(far, u, d)
        for dy in (1, 3, 2):
            remote(blk, blk, ys_sem, y1_rs.at[d, u, dy - 1], (0, dy, 0, 0))
        remote(blk, blk, cs_sem, c1_rs.at[d, u], (0, 0, 0, 1))

    def y1_arrive(d, u):
        for dy in (1, 3, 2):
            blk = lrows((((y - dy) % 4) * 2 + (1 - zh)) * 2 + c, u, d)
            wait(blk, y1_rs.at[d, u, dy - 1])
            remote(blk, blk, cs_sem, c1_rs.at[d, u], (0, 0, 0, 1))

    def mat(rows, zhalf):
        t = acc[rows, :]
        for yy in range(4):
            b = (yy * 2 + zhalf) * 2
            k = jnp.concatenate([L[b, rows, :], L[b + 1, rows, :]], axis=1)
            w = F[pl.ds(pl.multiple_of(b * CB, 2 * CB), 2 * CB), :]
            t = t + jnp.dot(k, w, preferred_element_type=jnp.float32)
        return t

    extra = {}

    def at(step, fn):
        extra.setdefault(step, []).append(fn)

    for k in range(len(SUM_STEPS)):
        at(k + 1, functools.partial(sum_step, k))
    at(len(SUM_STEPS) + 1, base)
    for i, dy in enumerate((1, 3, 2)):
        at(8 + i, functools.partial(y0_arrive, dy))
    for u in range(NU):
        for d in (0, 1):
            if u < NU - 1:
                at(LAM_START[u] + 8 + 3, functools.partial(y1_arrive, d, u))

    for t in range(1, STEPS + 1):
        for u in range(NU):
            h = t - LAM_START[u]
            if 0 <= h <= 8:
                for d in (0, 1):
                    if h > 0:
                        lam_wait(d, u, h - 1)
                    if h < 8:
                        lam_send(d, u, h)
                    else:
                        lam_final(d, u)
        for f in (0, 1):
            h = t - FOCK_START[f]
            if 0 <= h <= 7:
                for d in (0, 1):
                    if h == 0:
                        fock_send(d, f, 0)
                    else:
                        fock_arrive(d, f, h - 1)
        for fn in extra.pop(t, ()):
            fn()
    for t in sorted(extra):
        for fn in extra[t]:
            fn()

    wait(F.at[pl.ds(0, 24 * RA)], x_rs)
    wait(L.at[pl.ds(0, 4)], c0_rs)

    @pl.loop(0, PAIRS)
    def _(p):
        rows = pl.ds(pl.multiple_of(p * RA, RA), RA)
        acc[rows, :] = mat(rows, zh)

    for u in range(NU):
        if u == NU - 1:
            for d in (0, 1):
                y1_arrive(d, u)
        for d in (0, 1):
            wait(L.at[0, pl.ds(0, 4 * HALF)], c1_rs.at[d, u])
        rows = pl.ds(u * RA, RA)
        O[rows, :] = mat(rows, 1 - zh).astype(jnp.bfloat16)
        pltpu.make_async_copy(O.at[rows], out_ref.at[rows], out_sem.at[u]).start()

    wait(L.at[pl.ds(0, 8)], zs_sem)
    wait(L.at[pl.ds(0, 6)], xs_sem)
    wait(L.at[pl.ds(0, 6)], ys_sem)
    wait(L.at[pl.ds(0, 8)], cs_sem)
    for d in (0, 1):
        s = SG[d]
        for h in range(7):
            zsrc = zl - s * h

            @pl.when((zsrc >= 0) & (zsrc < 8) & (zl + s >= 0) & (zl + s < 8))
            def _(d=d, h=h):
                for f in (0, 1):
                    wait(F.at[pl.ds(0, HALF)], fock_ss.at[d, f, h])

    for k in range(len(SUM_STEPS)):
        wait(sbuf.at[k], sum_ss.at[k])
    for u in range(NU):
        rows = pl.ds(u * RA, RA)
        wait(O.at[rows], out_sem.at[u])


def body(lam, fock_vv, amp, tile_mask, integrals):
    bf16, f32 = jnp.bfloat16, jnp.float32
    dma = pltpu.SemaphoreType.DMA
    n = len(SUM_STEPS)
    anyspec = pl.BlockSpec(memory_space=pl.ANY)
    out = pl.pallas_call(
        kernel,
        name="residual",
        out_shape=jax.ShapeDtypeStruct((ROWS, CB), bf16),
        in_specs=[anyspec, anyspec, anyspec, pl.BlockSpec(memory_space=pltpu.SMEM), anyspec],
        out_specs=anyspec,
        scratch_shapes=[
            pltpu.VMEM((16, ROWS, CB), bf16),
            pltpu.VMEM((VIRT, CB), bf16),
            pltpu.VMEM((2, NU, 7, HALF, CB), bf16),
            pltpu.VMEM((ROWS, CB), bf16),
            pltpu.VMEM((ROWS, CB), bf16),
            pltpu.VMEM((ROWS, CB), f32),
            pltpu.VMEM((ROWS, CB), bf16),
            pltpu.VMEM((n + 1, 8, 128), f32),
            pltpu.VMEM((n, 8, 128), f32),
            dma((4,)),
            dma((2, NU, 8)),
            dma((2, 2, 7)),
            dma((2, 2, 7)),
            dma,
            dma((3,)),
            dma((2, NU, 3)),
            dma,
            dma((2, NU)),
            dma((n,)),
            dma((n,)),
            dma,
            dma,
            dma,
            dma,
            dma((NU,)),
        ],
        compiler_params=pltpu.CompilerParams(
            collective_id=0, has_side_effects=True, vmem_limit_bytes=63 << 20
        ),
    )(lam.reshape(ROWS, CB), fock_vv, amp.reshape(ROWS, CB), tile_mask, integrals.reshape(ROWS, CB))
    return out.reshape(PAIRS, RA, CB)


def solution(mesh):
    split = P(None, "va", "vb")
    return jax.shard_map(
        body, mesh=mesh, in_specs=(split, P("va", "vb"), split, split, split), out_specs=split, check_vma=False
    )
```

```python
import functools

import jax
import jax.numpy as jnp
from jax import lax
from jax.experimental import pallas as pl
from jax.experimental.pallas import tpu as pltpu
from jax.sharding import PartitionSpec as P

VIRT = 6144
PAIRS = 4
RA = 192
CB = 384
ROWS = PAIRS * RA
HALF = RA // 2
MESH = pl.DeviceIdType.MESH

UNITS = ((64, 0), (64, 0), (64, 0), (64, 0), (64, 8), (64, 8))
PARTS = ((64, 0), (64, 7), (64, 8))
Y0_AT = 9
Y1_LAG = 5
INTER_AT = (0.2, 0.4)
SUM_AT = (2.5, 5.5, 8.5, 11.5)
LAST = max(t for _, t in UNITS)
NU, NF = len(UNITS), len(PARTS)
UOFF = tuple(sum(r for r, _ in UNITS[:u]) for u in range(NU + 1))
FOFF = tuple(sum(r for r, _ in PARTS[:f]) for f in range(NF + 1))

SUM_STAGES = (
    tuple((0, dy, 0, dc) for dc in (1, 0) for dy in (0, 1, 3, 2) if dy + dc),
    ((1, 0, 0, 0), (3, 0, 0, 0), (2, 0, 0, 0)),
    ((0, 0, 4, 0), (0, 0, 12, 0), (0, 0, 8, 0)),
    ((0, 0, 1, 0), (0, 0, 15, 0), (0, 0, 2, 0)),
)
NS = len(SUM_STAGES)


def kernel(
    lam_ref, fock_ref, amp_ref, mask_ref, int_ref, out_ref,
    L, F, T, A, I, acc, O, sbuf, rbuf,
    in_sem, lam_rs, fock_rs, fock_ss, x_rs, y0_rs, y1_rs, c0_rs, c1_rs, sum_rs, sum_ss,
    zs_sem, xs_sem, ys_sem, cs_sem, out_sem,
):
    va, vb = lax.axis_index("va"), lax.axis_index("vb")
    x, zl = va // 8, va % 8
    y, zh, c = vb // 4, (vb // 2) % 2, vb % 2
    z = zh * 8 + zl

    def dev(dx, dy, dz, dc):
        xx, yy, zz, cc = (x + dx) % 4, (y + dy) % 4, (z + dz) % 16, (c + dc) % 2
        return (xx * 8 + zz % 8, (yy * 2 + zz // 8) * 2 + cc)

    def remote(src, dst, ss, rs, to):
        pltpu.make_async_remote_copy(src, dst, ss, rs, device_id=dev(*to), device_id_type=MESH).start()

    def wait(ref, sem):
        pltpu.make_async_copy(ref, ref, sem).wait()

    own = vb
    far = (y * 2 + (1 - zh)) * 2 + c

    def frows(zsrc, f=None):
        base = (x * 8 + zsrc) * RA
        if f is None:
            return F.at[pl.ds(pl.multiple_of(base, RA), RA)]
        return F.at[pl.ds(pl.multiple_of(base + FOFF[f], 16), PARTS[f][0])]

    def lrows(b, u, d):
        return L.at[b, pl.ds(2 * UOFF[u] + d * UNITS[u][0], UNITS[u][0])]

    def urows(b, u):
        return L.at[b, pl.ds(2 * UOFF[u], 2 * UNITS[u][0])]

    def transit(d, u, h):
        return T.at[d, h, pl.ds(UOFF[u], UNITS[u][0])]

    cp_lam = pltpu.make_async_copy(lam_ref, L.at[own], in_sem.at[0])
    cp_fock = pltpu.make_async_copy(fock_ref, frows(zl), in_sem.at[1])
    cp_amp = pltpu.make_async_copy(amp_ref, A, in_sem.at[2])
    cp_int = pltpu.make_async_copy(int_ref, I, in_sem.at[3])
    cp_lam.start()
    cp_fock.start()
    cp_amp.start()
    cp_int.start()

    peers = set()
    for o in sum(SUM_STAGES, ()):
        peers.add(o)
        peers.add(((-o[0]) % 4, (-o[1]) % 4, (-o[2]) % 16, (-o[3]) % 2))
    peers = sorted(peers)
    bar = pltpu.get_barrier_semaphore()
    for o in peers:
        pl.semaphore_signal(bar, inc=1, device_id=dev(*o), device_id_type=MESH)
    pl.semaphore_wait(bar, len(peers))

    DZ = ((0, 0, 1, 0), (0, 0, -1, 0))
    SG = (1, -1)

    def lam_send(d, u, h):
        src = lrows(own, u, d) if h == 0 else transit(d, u, h - 1)
        if h < 7:
            dst = transit(d, u, h)
        else:
            zz = (z + SG[d]) % 16
            dst = lrows((y * 2 + (1 - zz // 8)) * 2 + c, u, d)
        remote(src, dst, zs_sem, lam_rs.at[d, u, h], DZ[d])

    def lam_wait(d, u, h):
        wait(transit(d, u, h) if h < 7 else lrows(far, u, d), lam_rs.at[d, u, h])

    def fock_send(d, f, h):
        s = SG[d]
        zsrc = zl - s * h

        @pl.when((zsrc >= 0) & (zsrc < 8) & (zl + s >= 0) & (zl + s < 8))
        def _():
            blk = frows(zsrc, f)
            remote(blk, blk, fock_ss.at[d, f, h], fock_rs.at[d, f, h], DZ[d])

    def fock_arrive(d, f, h):
        s = SG[d]
        zsrc = zl - s * (h + 1)

        @pl.when((zsrc >= 0) & (zsrc < 8))
        def _():
            blk = frows(zsrc, f)
            wait(blk, fock_rs.at[d, f, h])

        if h < 6:
            fock_send(d, f, h + 1)

        @pl.when((zsrc >= 0) & (zsrc < 8))
        def _():
            blk = frows(zsrc, f)
            for dx in (1, 3, 2):
                remote(blk, blk, xs_sem, x_rs, (dx, 0, 0, 0))

    cp_lam.wait()
    for u in range(NU):
        if UNITS[u][1] == 0:
            for d in (0, 1):
                lam_send(d, u, 0)
    cp_fock.wait()
    for f in range(NF):
        if PARTS[f][1] == 0:
            for d in (0, 1):
                fock_send(d, f, 0)
    blk = frows(zl)
    for dx in (1, 3, 2):
        remote(blk, blk, xs_sem, x_rs, (dx, 0, 0, 0))
    remote(L.at[own], L.at[own], cs_sem, c0_rs, (0, 0, 0, 1))
    def inter_part(i):
        if i == 0:
            cp_amp.wait()
        col = lax.broadcasted_iota(jnp.int32, (8, 128), 1)
        wide = []
        for q in range(PAIRS):
            kept = [mask_ref[q, i, j].astype(jnp.float32) for j in range(4)]
            wide.append(
                [jnp.where(col + g * 128 < (g + 1) * HALF, kept[g], kept[g + 1]) for g in range(3)]
            )

        def rows16(k, sums):
            sums = list(sums)
            r = pl.multiple_of(i * HALF + k * 16, 16)
            for g in range(3):
                lanes = pl.ds(g * 128, 128)
                a = [A[pl.ds(q * RA + r, 16), lanes].astype(jnp.float32) for q in range(PAIRS)]
                t = [L[own, pl.ds(p * RA + r, 16), lanes].astype(jnp.float32) for p in range(PAIRS)]
                for e in (0, 8):
                    for q in range(PAIRS):
                        m = a[q][e : e + 8] * wide[q][g]
                        for p in range(PAIRS):
                            sums[q * PAIRS + p] += t[p][e : e + 8] * m
            return tuple(sums)

        zeros = tuple(jnp.zeros((8, 128), jnp.float32) for _ in range(PAIRS * PAIRS))
        sums = lax.fori_loop(0, HALF // 16, rows16, zeros)
        rows = jnp.concatenate([jnp.sum(t, axis=0, keepdims=True) for t in sums], axis=0)
        part = jnp.broadcast_to(jnp.sum(rows, axis=1, keepdims=True), (PAIRS * PAIRS, 128))
        if i == 0:
            sbuf[0] = part
        else:
            sbuf[0] = sbuf[0] + part
            sum_send(0)
            for dy in (1, 3, 2):
                remote(L.at[own], L.at[own], ys_sem, y0_rs.at[dy - 1], (0, dy, 0, 0))

    def sum_send(k):
        for i, o in enumerate(SUM_STAGES[k]):
            remote(sbuf.at[k], rbuf.at[k, i], sum_ss.at[k], sum_rs.at[k], o)

    def sum_arrive(k):
        n = len(SUM_STAGES[k])
        wait(rbuf.at[k, pl.ds(0, n)], sum_rs.at[k])
        t = sbuf[k]
        for i in range(n):
            t = t + rbuf[k, i]
        sbuf[k + 1] = t
        if k + 1 < NS:
            sum_send(k + 1)

    def base():
        cp_int.wait()
        total = sbuf[NS] / VIRT
        inter = [
            [jnp.broadcast_to(total[q * PAIRS + p : q * PAIRS + p + 1, :], (16, 128)) for q in range(PAIRS)]
            for p in range(PAIRS)
        ]

        def rows16(k, carry):
            r = pl.multiple_of(k * 16, 16)
            for g in range(3):
                lanes = pl.ds(g * 128, 128)
                v = [I[pl.ds(q * RA + r, 16), lanes].astype(jnp.float32) for q in range(PAIRS)]
                for p in range(PAIRS):
                    t = v[p]
                    for q in range(PAIRS):
                        t = t + inter[p][q] * v[q]
                    acc[pl.ds(p * RA + r, 16), lanes] = t
            return carry

        lax.fori_loop(0, RA // 16, rows16, 0)

    def y0_arrive(dy):
        b = (((y - dy) % 4) * 2 + zh) * 2 + c
        wait(L.at[b], y0_rs.at[dy - 1])
        remote(L.at[b], L.at[b], cs_sem, c0_rs, (0, 0, 0, 1))

    def lam_final(u):
        blk = urows(far, u)
        for dy in (1, 3, 2):
            remote(blk, blk, ys_sem, y1_rs.at[u, dy - 1], (0, dy, 0, 0))
        remote(blk, blk, cs_sem, c1_rs.at[u], (0, 0, 0, 1))

    def y1_arrive(u):
        for dy in (1, 3, 2):
            blk = urows((((y - dy) % 4) * 2 + (1 - zh)) * 2 + c, u)
            wait(blk, y1_rs.at[u, dy - 1])
            remote(blk, blk, cs_sem, c1_rs.at[u], (0, 0, 0, 1))

    def mat(rows, zhalf):
        t = acc[rows, :]
        for yy in range(4):
            b = (yy * 2 + zhalf) * 2
            k = jnp.concatenate([L[b, rows, :], L[b + 1, rows, :]], axis=1)
            w = F[pl.ds(pl.multiple_of(b * CB, 2 * CB), 2 * CB), :]
            t = t + jnp.dot(k, w, preferred_element_type=jnp.float32)
        return t

    def near():
        wait(F.at[pl.ds(0, 24 * RA)], x_rs)
        wait(L.at[pl.ds(0, 4)], c0_rs)

        @pl.loop(0, PAIRS)
        def _(p):
            rows = pl.ds(pl.multiple_of(p * RA, RA), RA)
            acc[rows, :] = mat(rows, zh)

    def lam_step(u, h):
        for d in (0, 1):
            if h > 0:
                lam_wait(d, u, h - 1)
            if h < 8:
                lam_send(d, u, h)
        if h == 8:
            lam_final(u)

    def fock_step(f, h):
        for d in (0, 1):
            if h == 0:
                fock_send(d, f, 0)
            else:
                fock_arrive(d, f, h - 1)

    events = []

    def at(step, fn, *args):
        events.append((step, len(events), functools.partial(fn, *args)))

    for u in range(NU):
        for h in range(9):
            if UNITS[u][1] + h > 0:
                at(UNITS[u][1] + h, lam_step, u, h)
        at(LAST + 9 if UNITS[u][1] == LAST else UNITS[u][1] + 8 + Y1_LAG, y1_arrive, u)
    for f in range(NF):
        for h in range(8):
            if PARTS[f][1] + h > 0:
                at(PARTS[f][1] + h + 0.1, fock_step, f, h)
    for i in range(2):
        at(INTER_AT[i], inter_part, i)
    for k in range(NS):
        at(SUM_AT[k], sum_arrive, k)
    for i, dy in enumerate((1, 3, 2)):
        at(Y0_AT + 0.3 * i, y0_arrive, dy)
    at(LAST + 8.5, base)
    at(LAST + 8.6, near)
    for _, _, fn in sorted(events, key=lambda e: e[:2]):
        fn()

    for u in range(NU):
        wait(L.at[0, pl.ds(0, 8 * UNITS[u][0])], c1_rs.at[u])
        rows = pl.ds(2 * UOFF[u], 2 * UNITS[u][0])
        O[rows, :] = mat(rows, 1 - zh).astype(jnp.bfloat16)
        pltpu.make_async_copy(O.at[rows], out_ref.at[rows], out_sem.at[u]).start()

    wait(L.at[pl.ds(0, 8)], zs_sem)
    wait(L.at[pl.ds(0, 6)], xs_sem)
    wait(L.at[pl.ds(0, 6)], ys_sem)
    wait(L.at[pl.ds(0, 8)], cs_sem)
    for d in (0, 1):
        s = SG[d]
        for h in range(7):
            zsrc = zl - s * h

            @pl.when((zsrc >= 0) & (zsrc < 8) & (zl + s >= 0) & (zl + s < 8))
            def _(d=d, h=h):
                for f in range(NF):
                    wait(F.at[pl.ds(0, PARTS[f][0])], fock_ss.at[d, f, h])

    for k in range(NS):
        wait(rbuf.at[k, pl.ds(0, len(SUM_STAGES[k]))], sum_ss.at[k])
    for u in range(NU):
        rows = pl.ds(2 * UOFF[u], 2 * UNITS[u][0])
        wait(O.at[rows], out_sem.at[u])


def body(lam, fock_vv, amp, tile_mask, integrals):
    bf16, f32 = jnp.bfloat16, jnp.float32
    dma = pltpu.SemaphoreType.DMA
    anyspec = pl.BlockSpec(memory_space=pl.ANY)
    out = pl.pallas_call(
        kernel,
        name="residual",
        out_shape=jax.ShapeDtypeStruct((ROWS, CB), bf16),
        in_specs=[anyspec, anyspec, anyspec, pl.BlockSpec(memory_space=pltpu.SMEM), anyspec],
        out_specs=anyspec,
        scratch_shapes=[
            pltpu.VMEM((16, ROWS, CB), bf16),
            pltpu.VMEM((VIRT, CB), bf16),
            pltpu.VMEM((2, 7, ROWS // 2, CB), bf16),
            pltpu.VMEM((ROWS, CB), bf16),
            pltpu.VMEM((ROWS, CB), bf16),
            pltpu.VMEM((ROWS, CB), f32),
            pltpu.VMEM((ROWS, CB), bf16),
            pltpu.VMEM((NS + 1, PAIRS * PAIRS, 128), f32),
            pltpu.VMEM((NS, 7, PAIRS * PAIRS, 128), f32),
            dma((4,)),
            dma((2, NU, 8)),
            dma((2, NF, 7)),
            dma((2, NF, 7)),
            dma,
            dma((3,)),
            dma((NU, 3)),
            dma,
            dma((NU,)),
            dma((NS,)),
            dma((NS,)),
            dma,
            dma,
            dma,
            dma,
            dma((NU,)),
        ],
        compiler_params=pltpu.CompilerParams(
            collective_id=0, has_side_effects=True, vmem_limit_bytes=63 << 20
        ),
    )(lam.reshape(ROWS, CB), fock_vv, amp.reshape(ROWS, CB), tile_mask, integrals.reshape(ROWS, CB))
    return out.reshape(PAIRS, RA, CB)


def solution(mesh):
    split = P(None, "va", "vb")
    return jax.shard_map(
        body, mesh=mesh, in_specs=(split, P("va", "vb"), split, split, split), out_specs=split, check_vma=False
    )
```

```python
import functools

import jax
import jax.numpy as jnp
from jax import lax
from jax.experimental import pallas as pl
from jax.experimental.pallas import tpu as pltpu
from jax.sharding import PartitionSpec as P

VIRT = 6144
PAIRS = 4
RA = 192
CB = 384
ROWS = PAIRS * RA
HALF = RA // 2
MESH = pl.DeviceIdType.MESH

UNITS = ((64, 0), (64, 0), (64, 0), (64, 0), (64, 7), (64, 7))
PARTS = ((64, 0), (64, 7), (64, 8))
Y0_AT = 9
Y1_LAG = 5
INTER_AT = (0.2, 0.4)
SUM_AT = (1.2, 3.5, 6.5, 9.5, 12.5)
LAST = max(t for _, t in UNITS)
NU, NF = len(UNITS), len(PARTS)
UOFF = tuple(sum(r for r, _ in UNITS[:u]) for u in range(NU + 1))
FOFF = tuple(sum(r for r, _ in PARTS[:f]) for f in range(NF + 1))

SUM_STAGES = (
    ((0, 0, 0, 1),),
    ((0, 1, 0, 0), (0, 3, 0, 0), (0, 2, 0, 0)),
    ((1, 0, 0, 0), (3, 0, 0, 0), (2, 0, 0, 0)),
    ((0, 0, 4, 0), (0, 0, 12, 0), (0, 0, 8, 0)),
    ((0, 0, 1, 0), (0, 0, 15, 0), (0, 0, 2, 0)),
)
NS = len(SUM_STAGES)


def kernel(
    lam_ref, fock_ref, amp_ref, mask_ref, int_ref, out_ref,
    L, F, T, A, I, acc, O, sbuf, rbuf,
    in_sem, lam_rs, fock_rs, fock_ss, x_rs, y0_rs, y1_rs, c0_rs, c1_rs, sum_rs, sum_ss,
    zs_sem, xs_sem, ys_sem, cs_sem, out_sem,
):
    va, vb = lax.axis_index("va"), lax.axis_index("vb")
    x, zl = lax.div(va, 8), lax.rem(va, 8)
    y, zh, c = lax.div(vb, 4), lax.rem(lax.div(vb, 2), 2), lax.rem(vb, 2)
    z = zh * 8 + zl
    ids = {}

    def dev(dx, dy, dz, dc):
        o = (dx, dy, dz, dc)
        if o not in ids:
            a, b = va, vb
            if dx:
                a = a + (lax.rem(x + dx, 4) - x) * 8
            if dy:
                b = b + (lax.rem(y + dy, 4) - y) * 4
            if dz:
                zz = lax.rem(z + dz, 16)
                a, b = a + lax.rem(zz, 8) - zl, b + (lax.div(zz, 8) - zh) * 2
            if dc:
                b = b + 1 - 2 * c
            ids[o] = (a, b)
        return ids[o]

    def remote(src, dst, ss, rs, to):
        pltpu.make_async_remote_copy(src, dst, ss, rs, device_id=dev(*to), device_id_type=MESH).start()

    def wait(ref, sem):
        pltpu.make_async_copy(ref, ref, sem).wait()

    own = vb
    far = (y * 2 + (1 - zh)) * 2 + c

    def frows(zsrc, f=None):
        base = (x * 8 + zsrc) * RA
        if f is None:
            return F.at[pl.ds(pl.multiple_of(base, RA), RA)]
        return F.at[pl.ds(pl.multiple_of(base + FOFF[f], 16), PARTS[f][0])]

    def lrows(b, u, d):
        return L.at[b, pl.ds(2 * UOFF[u] + d * UNITS[u][0], UNITS[u][0])]

    def urows(b, u):
        return L.at[b, pl.ds(2 * UOFF[u], 2 * UNITS[u][0])]

    def transit(d, u, h):
        return T.at[d, h, pl.ds(UOFF[u], UNITS[u][0])]

    cp_lam = pltpu.make_async_copy(lam_ref, L.at[own], in_sem.at[0])
    cp_fock = pltpu.make_async_copy(fock_ref, frows(zl), in_sem.at[1])
    cp_amp = pltpu.make_async_copy(amp_ref, A, in_sem.at[2])
    cp_int = pltpu.make_async_copy(int_ref, I, in_sem.at[3])
    cp_lam.start()
    cp_fock.start()
    cp_amp.start()
    cp_int.start()

    peers = set()
    for o in sum(SUM_STAGES, ()):
        peers.add(o)
        peers.add(((-o[0]) % 4, (-o[1]) % 4, (-o[2]) % 16, (-o[3]) % 2))
    peers = sorted(peers)
    bar = pltpu.get_barrier_semaphore()
    for o in peers:
        pl.semaphore_signal(bar, inc=1, device_id=dev(*o), device_id_type=MESH)
    pl.semaphore_wait(bar, len(peers))

    DZ = ((0, 0, 1, 0), (0, 0, 15, 0))
    SG = (1, -1)

    def lam_send(d, u, h):
        src = lrows(own, u, d) if h == 0 else transit(d, u, h - 1)
        if h < 7:
            dst = transit(d, u, h)
        else:
            zz = lax.rem(z + DZ[d][2], 16)
            dst = lrows((y * 2 + (1 - lax.div(zz, 8))) * 2 + c, u, d)
        remote(src, dst, zs_sem, lam_rs.at[d, u, h], DZ[d])

    def lam_wait(d, u, h):
        wait(transit(d, u, h) if h < 7 else lrows(far, u, d), lam_rs.at[d, u, h])

    def fock_send(d, f, h):
        s = SG[d]
        zsrc = zl - s * h

        @pl.when((zsrc >= 0) & (zsrc < 8) & (zl + s >= 0) & (zl + s < 8))
        def _():
            blk = frows(zsrc, f)
            remote(blk, blk, fock_ss.at[d, f, h], fock_rs.at[d, f, h], DZ[d])

    def fock_arrive(d, f, h):
        s = SG[d]
        zsrc = zl - s * (h + 1)

        @pl.when((zsrc >= 0) & (zsrc < 8))
        def _():
            blk = frows(zsrc, f)
            wait(blk, fock_rs.at[d, f, h])

        if h < 6:
            fock_send(d, f, h + 1)

        @pl.when((zsrc >= 0) & (zsrc < 8))
        def _():
            blk = frows(zsrc, f)
            for dx in (1, 3, 2):
                remote(blk, blk, xs_sem, x_rs, (dx, 0, 0, 0))

    cp_lam.wait()
    for u in range(NU):
        if UNITS[u][1] == 0:
            for d in (0, 1):
                lam_send(d, u, 0)
    cp_fock.wait()
    for f in range(NF):
        if PARTS[f][1] == 0:
            for d in (0, 1):
                fock_send(d, f, 0)
    blk = frows(zl)
    for dx in (1, 3, 2):
        remote(blk, blk, xs_sem, x_rs, (dx, 0, 0, 0))
    remote(L.at[own], L.at[own], cs_sem, c0_rs, (0, 0, 0, 1))
    def inter_part(i):
        if i == 0:
            cp_amp.wait()
        col = lax.broadcasted_iota(jnp.int32, (8, 128), 1)
        wide = []
        for q in range(PAIRS):
            kept = [mask_ref[q, i, j].astype(jnp.float32) for j in range(4)]
            wide.append(
                [jnp.where(col + g * 128 < (g + 1) * HALF, kept[g], kept[g + 1]) for g in range(3)]
            )

        def rows16(k, sums):
            sums = list(sums)
            r = pl.multiple_of(i * HALF + k * 16, 16)
            for g in range(3):
                lanes = pl.ds(g * 128, 128)
                a = [A[pl.ds(q * RA + r, 16), lanes].astype(jnp.float32) for q in range(PAIRS)]
                t = [L[own, pl.ds(p * RA + r, 16), lanes].astype(jnp.float32) for p in range(PAIRS)]
                for e in (0, 8):
                    for q in range(PAIRS):
                        m = a[q][e : e + 8] * wide[q][g]
                        for p in range(PAIRS):
                            sums[q * PAIRS + p] += t[p][e : e + 8] * m
            return tuple(sums)

        zeros = tuple(jnp.zeros((8, 128), jnp.float32) for _ in range(PAIRS * PAIRS))
        sums = lax.fori_loop(0, HALF // 16, rows16, zeros)
        rows = jnp.concatenate([jnp.sum(t, axis=0, keepdims=True) for t in sums], axis=0)
        part = jnp.broadcast_to(jnp.sum(rows, axis=1, keepdims=True), (PAIRS * PAIRS, 128))
        if i == 0:
            sbuf[0] = part
        else:
            sbuf[0] = sbuf[0] + part
            sum_send(0)

    def sum_send(k):
        for i, o in enumerate(SUM_STAGES[k]):
            remote(sbuf.at[k], rbuf.at[k, i], sum_ss.at[k], sum_rs.at[k], o)

    def sum_arrive(k):
        n = len(SUM_STAGES[k])
        wait(rbuf.at[k, pl.ds(0, n)], sum_rs.at[k])
        t = sbuf[k]
        for i in range(n):
            t = t + rbuf[k, i]
        sbuf[k + 1] = t
        if k + 1 < NS:
            sum_send(k + 1)
        if k == 0:
            for dy in (1, 3, 2):
                remote(L.at[own], L.at[own], ys_sem, y0_rs.at[dy - 1], (0, dy, 0, 0))

    def base():
        cp_int.wait()
        total = sbuf[NS] / VIRT
        inter = [
            [jnp.broadcast_to(total[q * PAIRS + p : q * PAIRS + p + 1, :], (16, 128)) for q in range(PAIRS)]
            for p in range(PAIRS)
        ]

        def rows16(k, carry):
            r = pl.multiple_of(k * 16, 16)
            for g in range(3):
                lanes = pl.ds(g * 128, 128)
                v = [I[pl.ds(q * RA + r, 16), lanes].astype(jnp.float32) for q in range(PAIRS)]
                for p in range(PAIRS):
                    t = v[p]
                    for q in range(PAIRS):
                        t = t + inter[p][q] * v[q]
                    acc[pl.ds(p * RA + r, 16), lanes] = t
            return carry

        lax.fori_loop(0, RA // 16, rows16, 0)

    def y0_arrive(dy):
        b = (lax.rem(y + 4 - dy, 4) * 2 + zh) * 2 + c
        wait(L.at[b], y0_rs.at[dy - 1])
        remote(L.at[b], L.at[b], cs_sem, c0_rs, (0, 0, 0, 1))

    def lam_final(u):
        blk = urows(far, u)
        for dy in (1, 3, 2):
            remote(blk, blk, ys_sem, y1_rs.at[u, dy - 1], (0, dy, 0, 0))
        remote(blk, blk, cs_sem, c1_rs.at[u], (0, 0, 0, 1))

    def y1_arrive(u):
        for dy in (1, 3, 2):
            blk = urows((lax.rem(y + 4 - dy, 4) * 2 + (1 - zh)) * 2 + c, u)
            wait(blk, y1_rs.at[u, dy - 1])
            remote(blk, blk, cs_sem, c1_rs.at[u], (0, 0, 0, 1))

    def mat(rows, zhalf):
        t = acc[rows, :]
        for yy in range(4):
            b = (yy * 2 + zhalf) * 2
            k = jnp.concatenate([L[b, rows, :], L[b + 1, rows, :]], axis=1)
            w = F[pl.ds(pl.multiple_of(b * CB, 2 * CB), 2 * CB), :]
            t = t + jnp.dot(k, w, preferred_element_type=jnp.float32)
        return t

    def near():
        wait(F.at[pl.ds(0, 24 * RA)], x_rs)
        wait(L.at[pl.ds(0, 4)], c0_rs)

        @pl.loop(0, PAIRS)
        def _(p):
            rows = pl.ds(pl.multiple_of(p * RA, RA), RA)
            acc[rows, :] = mat(rows, zh)

    def lam_step(u, h):
        for d in (0, 1):
            if h > 0:
                lam_wait(d, u, h - 1)
            if h < 8:
                lam_send(d, u, h)
        if h == 8:
            lam_final(u)

    def fock_step(f, h):
        for d in (0, 1):
            if h == 0:
                fock_send(d, f, 0)
            else:
                fock_arrive(d, f, h - 1)

    events = []

    def at(step, fn, *args):
        events.append((step, len(events), functools.partial(fn, *args)))

    for u in range(NU):
        for h in range(9):
            if UNITS[u][1] + h > 0:
                at(UNITS[u][1] + h, lam_step, u, h)
        at(LAST + 9 if UNITS[u][1] == LAST else UNITS[u][1] + 8 + Y1_LAG, y1_arrive, u)
    for f in range(NF):
        for h in range(8):
            if PARTS[f][1] + h > 0:
                at(PARTS[f][1] + h + 0.1, fock_step, f, h)
    for i in range(2):
        at(INTER_AT[i], inter_part, i)
    for k in range(NS):
        at(SUM_AT[k], sum_arrive, k)
    for i, dy in enumerate((1, 3, 2)):
        at(Y0_AT + 0.3 * i, y0_arrive, dy)
    at(LAST + 8.5, base)
    at(max(LAST + 8.6, max(t for _, t in PARTS) + 7.2), near)
    for _, _, fn in sorted(events, key=lambda e: e[:2]):
        fn()

    for u in range(NU):
        wait(L.at[0, pl.ds(0, 8 * UNITS[u][0])], c1_rs.at[u])
        rows = pl.ds(2 * UOFF[u], 2 * UNITS[u][0])
        O[rows, :] = mat(rows, 1 - zh).astype(jnp.bfloat16)
        pltpu.make_async_copy(O.at[rows], out_ref.at[rows], out_sem.at[u]).start()

    wait(L.at[pl.ds(0, 8)], zs_sem)
    wait(L.at[pl.ds(0, 6)], xs_sem)
    wait(L.at[pl.ds(0, 6)], ys_sem)
    wait(L.at[pl.ds(0, 8)], cs_sem)
    for d in (0, 1):
        s = SG[d]
        for h in range(7):
            zsrc = zl - s * h

            @pl.when((zsrc >= 0) & (zsrc < 8) & (zl + s >= 0) & (zl + s < 8))
            def _(d=d, h=h):
                for f in range(NF):
                    wait(F.at[pl.ds(0, PARTS[f][0])], fock_ss.at[d, f, h])

    for k in range(NS):
        wait(rbuf.at[k, pl.ds(0, len(SUM_STAGES[k]))], sum_ss.at[k])
    for u in range(NU):
        rows = pl.ds(2 * UOFF[u], 2 * UNITS[u][0])
        wait(O.at[rows], out_sem.at[u])


def body(lam, fock_vv, amp, tile_mask, integrals):
    bf16, f32 = jnp.bfloat16, jnp.float32
    dma = pltpu.SemaphoreType.DMA
    anyspec = pl.BlockSpec(memory_space=pl.ANY)
    out = pl.pallas_call(
        kernel,
        name="residual",
        out_shape=jax.ShapeDtypeStruct((ROWS, CB), bf16),
        in_specs=[anyspec, anyspec, anyspec, pl.BlockSpec(memory_space=pltpu.SMEM), anyspec],
        out_specs=anyspec,
        scratch_shapes=[
            pltpu.VMEM((16, ROWS, CB), bf16),
            pltpu.VMEM((VIRT, CB), bf16),
            pltpu.VMEM((2, 7, ROWS // 2, CB), bf16),
            pltpu.VMEM((ROWS, CB), bf16),
            pltpu.VMEM((ROWS, CB), bf16),
            pltpu.VMEM((ROWS, CB), f32),
            pltpu.VMEM((ROWS, CB), bf16),
            pltpu.VMEM((NS + 1, PAIRS * PAIRS, 128), f32),
            pltpu.VMEM((NS, 3, PAIRS * PAIRS, 128), f32),
            dma((4,)),
            dma((2, NU, 8)),
            dma((2, NF, 7)),
            dma((2, NF, 7)),
            dma,
            dma((3,)),
            dma((NU, 3)),
            dma,
            dma((NU,)),
            dma((NS,)),
            dma((NS,)),
            dma,
            dma,
            dma,
            dma,
            dma((NU,)),
        ],
        compiler_params=pltpu.CompilerParams(
            collective_id=0, has_side_effects=True, vmem_limit_bytes=63 << 20
        ),
    )(lam.reshape(ROWS, CB), fock_vv, amp.reshape(ROWS, CB), tile_mask, integrals.reshape(ROWS, CB))
    return out.reshape(PAIRS, RA, CB)


def solution(mesh):
    split = P(None, "va", "vb")
    return jax.shard_map(
        body, mesh=mesh, in_specs=(split, P("va", "vb"), split, split, split), out_specs=split, check_vma=False
    )
```

```python
import functools

import jax
import jax.numpy as jnp
from jax import lax
from jax.experimental import pallas as pl
from jax.experimental.pallas import tpu as pltpu
from jax.sharding import PartitionSpec as P

VIRT = 6144
PAIRS = 4
RA = 192
CB = 384
ROWS = PAIRS * RA
HALF = RA // 2
MESH = pl.DeviceIdType.MESH

UNITS = ((64, 0), (64, 0), (64, 0), (64, 0), (64, 7), (64, 7))
PARTS = ((64, 0), (64, 7), (64, 8))
Y0_AT = 9
Y1_LAG = 5
INTER_AT = (0.2, 0.4)
SUM_AT = (1.2, 3.5, 6.5, 9.5, 12.5)
LAST = max(t for _, t in UNITS)
NU, NF = len(UNITS), len(PARTS)
UOFF = tuple(sum(r for r, _ in UNITS[:u]) for u in range(NU + 1))
FOFF = tuple(sum(r for r, _ in PARTS[:f]) for f in range(NF + 1))

SUM_STAGES = (
    ((0, 0, 0, 1),),
    ((0, 1, 0, 0), (0, 3, 0, 0), (0, 2, 0, 0)),
    ((1, 0, 0, 0), (3, 0, 0, 0), (2, 0, 0, 0)),
    ((0, 0, 4, 0), (0, 0, 12, 0), (0, 0, 8, 0)),
    ((0, 0, 1, 0), (0, 0, 15, 0), (0, 0, 2, 0)),
)
NS = len(SUM_STAGES)


def kernel(
    lam_ref, fock_ref, amp_ref, mask_ref, int_ref, out_ref,
    L, F, T, A, I, acc, O, sbuf, rbuf,
    in_sem, lam_rs, fock_rs, fock_ss, x_rs, y0_rs, y1_rs, c0_rs, c1_rs, sum_rs, sum_ss,
    zs_sem, xs_sem, ys_sem, cs_sem, out_sem,
):
    va, vb = lax.axis_index("va"), lax.axis_index("vb")
    x, zl = lax.div(va, 8), lax.rem(va, 8)
    y, zh, c = lax.div(vb, 4), lax.rem(lax.div(vb, 2), 2), lax.rem(vb, 2)
    z = zh * 8 + zl
    ids = {}

    def dev(dx, dy, dz, dc):
        o = (dx, dy, dz, dc)
        if o not in ids:
            a, b = va, vb
            if dx:
                a = a + (lax.rem(x + dx, 4) - x) * 8
            if dy:
                b = b + (lax.rem(y + dy, 4) - y) * 4
            if dz:
                zz = lax.rem(z + dz, 16)
                a, b = a + lax.rem(zz, 8) - zl, b + (lax.div(zz, 8) - zh) * 2
            if dc:
                b = b + 1 - 2 * c
            ids[o] = (a, b)
        return ids[o]

    def remote(src, dst, ss, rs, to):
        pltpu.make_async_remote_copy(src, dst, ss, rs, device_id=dev(*to), device_id_type=MESH).start()

    def wait(ref, sem):
        pltpu.make_async_copy(ref, ref, sem).wait()

    own = vb
    far = (y * 2 + (1 - zh)) * 2 + c

    def frows(zsrc, f=None):
        base = (x * 8 + zsrc) * RA
        if f is None:
            return F.at[pl.ds(pl.multiple_of(base, RA), RA)]
        return F.at[pl.ds(pl.multiple_of(base + FOFF[f], 16), PARTS[f][0])]

    def lrows(b, u, d):
        return L.at[b, pl.ds(2 * UOFF[u] + d * UNITS[u][0], UNITS[u][0])]

    def urows(b, u):
        return L.at[b, pl.ds(2 * UOFF[u], 2 * UNITS[u][0])]

    def transit(d, u, h):
        return T.at[d, h, pl.ds(UOFF[u], UNITS[u][0])]

    cp_lam = pltpu.make_async_copy(lam_ref, L.at[own], in_sem.at[0])
    cp_fock = pltpu.make_async_copy(fock_ref, frows(zl), in_sem.at[1])
    cp_amp = pltpu.make_async_copy(amp_ref, A, in_sem.at[2])
    cp_int = pltpu.make_async_copy(int_ref, I, in_sem.at[3])
    cp_lam.start()
    cp_fock.start()
    cp_amp.start()
    cp_int.start()

    peers = set()
    for o in sum(SUM_STAGES, ()):
        peers.add(o)
        peers.add(((-o[0]) % 4, (-o[1]) % 4, (-o[2]) % 16, (-o[3]) % 2))
    peers = sorted(peers)
    bar = pltpu.get_barrier_semaphore()
    for o in peers:
        pl.semaphore_signal(bar, inc=1, device_id=dev(*o), device_id_type=MESH)
    pl.semaphore_wait(bar, len(peers))

    DZ = ((0, 0, 1, 0), (0, 0, 15, 0))
    SG = (1, -1)

    def lam_send(d, u, h):
        src = lrows(own, u, d) if h == 0 else transit(d, u, h - 1)
        if h < 7:
            dst = transit(d, u, h)
        else:
            zz = lax.rem(z + DZ[d][2], 16)
            dst = lrows((y * 2 + (1 - lax.div(zz, 8))) * 2 + c, u, d)
        remote(src, dst, zs_sem, lam_rs.at[d, u, h], DZ[d])

    def lam_wait(d, u, h):
        wait(transit(d, u, h) if h < 7 else lrows(far, u, d), lam_rs.at[d, u, h])

    def fock_send(d, f, h):
        s = SG[d]
        zsrc = zl - s * h

        @pl.when((zsrc >= 0) & (zsrc < 8) & (zl + s >= 0) & (zl + s < 8))
        def _():
            blk = frows(zsrc, f)
            remote(blk, blk, fock_ss.at[d, f, h], fock_rs.at[d, f, h], DZ[d])

    def fock_arrive(d, f, h):
        s = SG[d]
        zsrc = zl - s * (h + 1)

        @pl.when((zsrc >= 0) & (zsrc < 8))
        def _():
            blk = frows(zsrc, f)
            wait(blk, fock_rs.at[d, f, h])

        if h < 6:
            fock_send(d, f, h + 1)

        @pl.when((zsrc >= 0) & (zsrc < 8))
        def _():
            blk = frows(zsrc, f)
            for dx in (1, 3, 2):
                remote(blk, blk, xs_sem, x_rs, (dx, 0, 0, 0))

    cp_lam.wait()
    for u in range(NU):
        if UNITS[u][1] == 0:
            for d in (0, 1):
                lam_send(d, u, 0)
    cp_fock.wait()
    for f in range(NF):
        if PARTS[f][1] == 0:
            for d in (0, 1):
                fock_send(d, f, 0)
    blk = frows(zl)
    for dx in (1, 3, 2):
        remote(blk, blk, xs_sem, x_rs, (dx, 0, 0, 0))
    remote(L.at[own], L.at[own], cs_sem, c0_rs, (0, 0, 0, 1))
    def inter_part(i):
        if i == 0:
            cp_amp.wait()
        col = lax.broadcasted_iota(jnp.int32, (8, 128), 1)
        wide = []
        for q in range(PAIRS):
            kept = [mask_ref[q, i, j].astype(jnp.float32) for j in range(4)]
            wide.append(
                [jnp.where(col + g * 128 < (g + 1) * HALF, kept[g], kept[g + 1]) for g in range(3)]
            )

        def rows16(k, sums):
            sums = list(sums)
            r = pl.multiple_of(i * HALF + k * 16, 16)
            for g in range(3):
                lanes = pl.ds(g * 128, 128)
                a = [A[pl.ds(q * RA + r, 16), lanes].astype(jnp.float32) for q in range(PAIRS)]
                t = [L[own, pl.ds(p * RA + r, 16), lanes].astype(jnp.float32) for p in range(PAIRS)]
                for e in (0, 8):
                    for q in range(PAIRS):
                        m = a[q][e : e + 8] * wide[q][g]
                        for p in range(PAIRS):
                            sums[q * PAIRS + p] += t[p][e : e + 8] * m
            return tuple(sums)

        zeros = tuple(jnp.zeros((8, 128), jnp.float32) for _ in range(PAIRS * PAIRS))
        sums = lax.fori_loop(0, HALF // 16, rows16, zeros)
        rows = jnp.concatenate([jnp.sum(t, axis=0, keepdims=True) for t in sums], axis=0)
        part = jnp.broadcast_to(jnp.sum(rows, axis=1, keepdims=True), (PAIRS * PAIRS, 128))
        if i == 0:
            sbuf[0] = part
        else:
            sbuf[0] = sbuf[0] + part
            sum_send(0)

    def sum_send(k):
        for i, o in enumerate(SUM_STAGES[k]):
            remote(sbuf.at[k], rbuf.at[k, i], sum_ss.at[k], sum_rs.at[k], o)

    def sum_arrive(k):
        n = len(SUM_STAGES[k])
        wait(rbuf.at[k, pl.ds(0, n)], sum_rs.at[k])
        t = sbuf[k]
        for i in range(n):
            t = t + rbuf[k, i]
        sbuf[k + 1] = t
        if k + 1 < NS:
            sum_send(k + 1)
        if k == 0:
            for dy in (1, 3, 2):
                remote(L.at[own], L.at[own], ys_sem, y0_rs.at[dy - 1], (0, dy, 0, 0))

    def base():
        cp_int.wait()
        total = sbuf[NS] / VIRT
        inter = [
            [jnp.broadcast_to(total[q * PAIRS + p : q * PAIRS + p + 1, :], (16, 128)) for q in range(PAIRS)]
            for p in range(PAIRS)
        ]

        def rows16(k, carry):
            r = pl.multiple_of(k * 16, 16)
            for g in range(3):
                lanes = pl.ds(g * 128, 128)
                v = [I[pl.ds(q * RA + r, 16), lanes].astype(jnp.float32) for q in range(PAIRS)]
                for p in range(PAIRS):
                    t = v[p]
                    for q in range(PAIRS):
                        t = t + inter[p][q] * v[q]
                    acc[pl.ds(p * RA + r, 16), lanes] = t
            return carry

        lax.fori_loop(0, RA // 16, rows16, 0)

    def y0_arrive(dy):
        b = (lax.rem(y + 4 - dy, 4) * 2 + zh) * 2 + c
        wait(L.at[b], y0_rs.at[dy - 1])
        remote(L.at[b], L.at[b], cs_sem, c0_rs, (0, 0, 0, 1))

    def lam_final(u):
        blk = urows(far, u)
        for dy in (2, 1, 3):
            remote(blk, blk, ys_sem, y1_rs.at[u, dy - 1], (0, dy, 0, 0))
        remote(blk, blk, cs_sem, c1_rs.at[u], (0, 0, 0, 1))

    def y1_arrive(u):
        for dy in (1, 3, 2):
            blk = urows((lax.rem(y + 4 - dy, 4) * 2 + (1 - zh)) * 2 + c, u)
            wait(blk, y1_rs.at[u, dy - 1])
            remote(blk, blk, cs_sem, c1_rs.at[u], (0, 0, 0, 1))

    def mat(rows, zhalf):
        t = acc[rows, :]
        for yy in range(4):
            b = (yy * 2 + zhalf) * 2
            k = jnp.concatenate([L[b, rows, :], L[b + 1, rows, :]], axis=1)
            w = F[pl.ds(pl.multiple_of(b * CB, 2 * CB), 2 * CB), :]
            t = t + jnp.dot(k, w, preferred_element_type=jnp.float32)
        return t

    def near():
        wait(F.at[pl.ds(0, 24 * RA)], x_rs)
        wait(L.at[pl.ds(0, 4)], c0_rs)

        @pl.loop(0, PAIRS)
        def _(p):
            rows = pl.ds(pl.multiple_of(p * RA, RA), RA)
            acc[rows, :] = mat(rows, zh)

    def lam_step(u, h):
        for d in (0, 1):
            if h > 0:
                lam_wait(d, u, h - 1)
            if h < 8:
                lam_send(d, u, h)
        if h == 8:
            lam_final(u)

    def fock_step(f, h):
        for d in (0, 1):
            if h == 0:
                fock_send(d, f, 0)
            else:
                fock_arrive(d, f, h - 1)

    events = []

    def at(step, fn, *args):
        events.append((step, len(events), functools.partial(fn, *args)))

    for u in range(NU):
        for h in range(9):
            if UNITS[u][1] + h > 0:
                at(UNITS[u][1] + h, lam_step, u, h)
        at(LAST + 9 if UNITS[u][1] == LAST else UNITS[u][1] + 8 + Y1_LAG, y1_arrive, u)
    for f in range(NF):
        for h in range(8):
            if PARTS[f][1] + h > 0:
                at(PARTS[f][1] + h + 0.1, fock_step, f, h)
    for i in range(2):
        at(INTER_AT[i], inter_part, i)
    for k in range(NS):
        at(SUM_AT[k], sum_arrive, k)
    for i, dy in enumerate((1, 3, 2)):
        at(Y0_AT + 0.3 * i, y0_arrive, dy)
    at(LAST + 8.5, base)
    at(max(LAST + 8.6, max(t for _, t in PARTS) + 7.2), near)
    for _, _, fn in sorted(events, key=lambda e: e[:2]):
        fn()

    for u in range(NU):
        wait(L.at[0, pl.ds(0, 8 * UNITS[u][0])], c1_rs.at[u])
        rows = pl.ds(2 * UOFF[u], 2 * UNITS[u][0])
        O[rows, :] = mat(rows, 1 - zh).astype(jnp.bfloat16)
        pltpu.make_async_copy(O.at[rows], out_ref.at[rows], out_sem.at[u]).start()

    wait(L.at[pl.ds(0, 8)], zs_sem)
    wait(L.at[pl.ds(0, 6)], xs_sem)
    wait(L.at[pl.ds(0, 6)], ys_sem)
    wait(L.at[pl.ds(0, 8)], cs_sem)
    for d in (0, 1):
        s = SG[d]
        for h in range(7):
            zsrc = zl - s * h

            @pl.when((zsrc >= 0) & (zsrc < 8) & (zl + s >= 0) & (zl + s < 8))
            def _(d=d, h=h):
                for f in range(NF):
                    wait(F.at[pl.ds(0, PARTS[f][0])], fock_ss.at[d, f, h])

    for k in range(NS):
        wait(rbuf.at[k, pl.ds(0, len(SUM_STAGES[k]))], sum_ss.at[k])
    for u in range(NU):
        rows = pl.ds(2 * UOFF[u], 2 * UNITS[u][0])
        wait(O.at[rows], out_sem.at[u])


def body(lam, fock_vv, amp, tile_mask, integrals):
    bf16, f32 = jnp.bfloat16, jnp.float32
    dma = pltpu.SemaphoreType.DMA
    anyspec = pl.BlockSpec(memory_space=pl.ANY)
    out = pl.pallas_call(
        kernel,
        name="residual",
        out_shape=jax.ShapeDtypeStruct((ROWS, CB), bf16),
        in_specs=[anyspec, anyspec, anyspec, pl.BlockSpec(memory_space=pltpu.SMEM), anyspec],
        out_specs=anyspec,
        scratch_shapes=[
            pltpu.VMEM((16, ROWS, CB), bf16),
            pltpu.VMEM((VIRT, CB), bf16),
            pltpu.VMEM((2, 7, ROWS // 2, CB), bf16),
            pltpu.VMEM((ROWS, CB), bf16),
            pltpu.VMEM((ROWS, CB), bf16),
            pltpu.VMEM((ROWS, CB), f32),
            pltpu.VMEM((ROWS, CB), bf16),
            pltpu.VMEM((NS + 1, PAIRS * PAIRS, 128), f32),
            pltpu.VMEM((NS, 3, PAIRS * PAIRS, 128), f32),
            dma((4,)),
            dma((2, NU, 8)),
            dma((2, NF, 7)),
            dma((2, NF, 7)),
            dma,
            dma((3,)),
            dma((NU, 3)),
            dma,
            dma((NU,)),
            dma((NS,)),
            dma((NS,)),
            dma,
            dma,
            dma,
            dma,
            dma((NU,)),
        ],
        compiler_params=pltpu.CompilerParams(
            collective_id=0, has_side_effects=True, vmem_limit_bytes=63 << 20
        ),
    )(lam.reshape(ROWS, CB), fock_vv, amp.reshape(ROWS, CB), tile_mask, integrals.reshape(ROWS, CB))
    return out.reshape(PAIRS, RA, CB)


def solution(mesh):
    split = P(None, "va", "vb")
    return jax.shard_map(
        body, mesh=mesh, in_specs=(split, P("va", "vb"), split, split, split), out_specs=split, check_vma=False
    )
```
